32 devices in a mesh: groups: 2 (over y), dp: 4 (over z), tensor: 2 (over x), sub: 2 (over core).
Axes of the slice: x: 2, y: 2, z: 4, core: 2. Of those that a mesh axis runs over, the one named last changes fastest.
Arguments:
- activations: bfloat16 [4096, 8192], P(('groups', 'dp'), ('tensor', 'sub')), parts along dimension 0, may hold values from -6 to 6
- cotangents: bfloat16 [4096, 28672], P(('groups', 'dp'), ('tensor', 'sub')), parts along dimension 0, may hold values from -0.125 to 0.125
- block_rows: int32 [4, 256], P(('tensor', 'sub')), may hold values from 0 to 127, as said below
- block_cols: int32 [4, 256], P(('tensor', 'sub')), may hold values from 0 to 111
- live_counts: int32 [4], P(('tensor', 'sub')), may hold values from 128 to 256, as said below
- owner_device: int32 [4, 256], replicated, may hold values from 0 to 15, as said below
- owner_slot: int32 [4, 256], replicated, may hold values from 0 to 63
Outputs:
- owned_grads: float32 [32, 64, 4096], P(('groups', 'dp', 'tensor', 'sub')), parts along dimension 0
The draws below stay inside these ranges and needn't reach their ends.
There are 2 independent parts, one for each index of `groups`. The reference program is written for one: setup_inputs(seed, part) draws one part's arguments, and reference() takes and returns one part's arrays. A program takes and returns all parts, laid end to end along the dimension named above; an argument that names none is the same for every part. Nothing has to cross between parts.
Inputs may be any that keep to these rules, and one draw needn't show every extreme that they name: Within one column group the pairs of block_rows and block_cols name distinct blocks. `live_counts`: some column group uses all 256 slots. `owner_device`: owner devices are numbered dp index times 4 plus column group. Each owner holds exactly 64 slots over all groups, one for each owner_slot value. Of one group's slots, exactly 64 have owners at each dp index, and these carry distinct owner_slot values. One group has at most 16 slots at one owner, and exactly 16 at some.
All inputs are finite; a program needn't handle non-finite values.
Results may differ from the reference program's by a relative error of at most 0.0003.
Values may be sent and summed in bfloat16 or wider, within the bound.
A program may use at most 128 MiB of HBM per device.

```python
import jax
import jax.numpy as jnp
from jax import lax

D = 8192
F = 28672
BS = 64
SLOTS = 256
N_COL = 4
TOKENS = 2048
FCOLS = 7168
RB = 128
CB = 112
OWNERS = 16
OWN_CAP = 64
TILE = 4096


def pattern(key):
    base_key = jax.random.fold_in(key, 11)
    picks = jax.vmap(lambda single: jax.random.permutation(single, RB * CB)[:SLOTS])(jax.random.split(base_key, N_COL))
    return picks.astype(jnp.int32)


def owners(key):
    base_key = jax.random.fold_in(key, 23)
    first_key, second_key, third_key = jax.random.split(base_key, 3)
    data_count = OWNERS // N_COL
    slot_order = jax.vmap(lambda single: jax.random.permutation(single, SLOTS))(jax.random.split(first_key, N_COL)).astype(jnp.int32)
    owner_data = slot_order // OWN_CAP
    owner_place = slot_order % OWN_CAP
    group_shift = jax.vmap(lambda single: jax.random.permutation(single, N_COL))(jax.random.split(second_key, data_count)).astype(jnp.int32)
    column_order = jax.vmap(lambda single: jax.random.permutation(single, N_COL))(jax.random.split(third_key, data_count)).astype(jnp.int32)
    group_index = jnp.broadcast_to(jnp.arange(N_COL, dtype=jnp.int32)[:, None], (N_COL, SLOTS))
    shifted = (group_shift[owner_data, group_index] + owner_place) % N_COL
    owner_column = column_order[owner_data, shifted]
    return ((owner_data * N_COL + owner_column).astype(jnp.int32), owner_place.astype(jnp.int32))


def draw_block_rows(key, part):
    return (pattern(key) // CB).astype(jnp.int32)


def draw_block_cols(key, part):
    return (pattern(key) % CB).astype(jnp.int32)


def draw_owner_device(key, part):
    return owners(key)[0]


def draw_owner_slot(key, part):
    return owners(key)[1]


def draw_live_counts(key, part):
    key = jax.random.fold_in(key, 37)
    first_key, second_key = jax.random.split(key, 2)
    counts = jax.random.randint(first_key, (N_COL,), SLOTS // 2, SLOTS + 1, dtype=jnp.int32)
    busiest = jax.random.randint(second_key, (), 0, N_COL, dtype=jnp.int32)
    return jnp.where(jnp.arange(N_COL, dtype=jnp.int32) == busiest, SLOTS, counts).astype(jnp.int32)


def steps_of(key, shape, cuts, smallest, largest):
    gain = 1.0
    for dim, shards_of in cuts:
        steps = jax.random.uniform(jax.random.fold_in(jax.random.fold_in(key, 6), dim), (shards_of,), jnp.float32, smallest / len(cuts), largest / len(cuts))
        gain = gain * jnp.repeat(jnp.exp(steps), shape[dim] // shards_of).reshape((-1,) + (1,) * (len(shape) - 1 - dim))
    return gain


def scatter_about(stream_key, extent, scale, reach, cuts=(), held_as=jnp.bfloat16):
    values = scale * jax.random.normal(stream_key, extent, jnp.float32)
    if cuts:
        values = values * steps_of(stream_key, extent, cuts, -0.22, 0.18)
    return jnp.clip(values, -reach, reach).astype(held_as)


def setup_inputs(seed: int = 0, part: int = 0) -> dict:
    arg_keys = jax.random.split(jax.random.key(seed), 8)
    part_splits = jax.random.split(jax.random.fold_in(arg_keys[7], part), 8)
    return {
        "activations": scatter_about(part_splits[0], (TOKENS, D), 1.0, 6.0, ((0, 4), (1, 4))),
        "cotangents": scatter_about(part_splits[1], (TOKENS, F), TOKENS ** -0.5, 0.125, ((0, 4), (1, 4))),
        "block_rows": draw_block_rows(jax.random.fold_in(arg_keys[7], 71), part),
        "block_cols": draw_block_cols(jax.random.fold_in(arg_keys[7], 71), part),
        "live_counts": draw_live_counts(jax.random.fold_in(arg_keys[7], 71), part),
        "owner_device": draw_owner_device(jax.random.fold_in(arg_keys[7], 71), part),
        "owner_slot": draw_owner_slot(jax.random.fold_in(arg_keys[7], 71), part),
    }


def reference(activations, cotangents, block_rows, block_cols, live_counts, owner_device, owner_slot):
    act_tiles = activations.astype(jnp.float32).reshape(TOKENS, RB, BS).transpose(1, 2, 0)
    block_width = min(32, SLOTS)
    blocks = SLOTS // block_width

    def per_group(group_index):
        cot_slice = lax.dynamic_slice_in_dim(cotangents, group_index * FCOLS, FCOLS, 1)
        cot_tiles = cot_slice.astype(jnp.float32).reshape(TOKENS, CB, BS).transpose(1, 2, 0)
        live_mask = jnp.arange(SLOTS, dtype=jnp.int32) < live_counts[group_index]

        def tile_block(pieces):
            row_ids, col_ids, keep_mask = pieces
            product = jnp.einsum("sat,sbt->sab", act_tiles[row_ids], cot_tiles[col_ids],
                                 precision=lax.Precision.HIGHEST)
            return jnp.where(keep_mask[:, None], product.reshape(block_width, TILE), 0.0)

        result = lax.map(tile_block, (block_rows[group_index].reshape(blocks, block_width),
                                      block_cols[group_index].reshape(blocks, block_width),
                                      live_mask.reshape(blocks, block_width)))
        return result.reshape(SLOTS, TILE)

    block_grads = lax.map(per_group, jnp.arange(N_COL, dtype=jnp.int32))
    owned = jnp.zeros((OWNERS, OWN_CAP, TILE), jnp.float32)
    owned = owned.at[owner_device.reshape(-1), owner_slot.reshape(-1)].set(block_grads.reshape(-1, TILE))
    return owned
```

```python
import functools

import jax
import jax.numpy as jnp
from jax import lax
from jax.experimental import pallas as pl
from jax.experimental.pallas import tpu as pltpu
from jax.sharding import PartitionSpec as P

BS = 64
HALF = 32
LANES = 128
QMAX = 32767.0
CHUNKS = 2
PIECES = 4
UNROLL = 8
MESH = pl.DeviceIdType.MESH


def kernel(
    ndp, nt, ns,
    code_ref, live_ref, src_ref, act_ref, cot_ref,
    out_ref,
    early, late, cotv, acc, sendq, sendc, recvq, recvc, total,
    cot_sem, local_sem, bsend, brecv, xsend, xrecv, fsend, frecv,
    qsend, qrecv, csend, crecv,
):
    ncol = nt * ns
    dp = lax.axis_index("dp")
    ti = lax.axis_index("tensor")
    si = lax.axis_index("sub")
    my_col = ti * ns + si
    me = dp * ncol + my_col
    owners = ndp * ncol
    feats = act_ref.shape[1]
    depth = act_ref.shape[3]
    piece = feats // PIECES
    stripes = cotv.shape[0]
    slots = acc.shape[0]
    gath = (early, late)
    pair = slots // owners

    def at(dev):
        return {"dp": dev // ncol, "tensor": lax.rem(dev, ncol) // ns, "sub": lax.rem(dev, ns)}

    def held(k, col, p=None):
        if p is None:
            return gath[k].at[pl.ds(col * feats, feats)]
        return gath[k].at[pl.ds(col * feats + p * piece, piece)]

    def stripe(i):
        return pltpu.make_async_copy(
            cot_ref.at[:, pl.ds(pl.multiple_of(i * LANES, LANES), LANES)], cotv.at[i], cot_sem.at[i]
        )

    def load(i, carry):
        stripe(i).start()
        return carry

    lax.fori_loop(0, stripes, load, 0)
    own_copies = [
        pltpu.make_async_copy(act_ref.at[k], held(k, my_col), local_sem.at[1 + k]) for k in range(CHUNKS)
    ]
    for copy in own_copies:
        copy.start()

    barrier = pltpu.get_barrier_semaphore()

    def greet(i, carry):
        dev = lax.rem(me + i, owners)
        pl.semaphore_signal(barrier, inc=1, device_id=at(dev), device_id_type=MESH)
        return carry

    lax.fori_loop(1, owners, greet, 0)
    pl.semaphore_wait(barrier, owners - 1)

    def across(o, k, p):
        return pltpu.make_async_remote_copy(
            src_ref=act_ref.at[k, pl.ds(p * piece, piece)],
            dst_ref=held(k, my_col, p),
            send_sem=xsend.at[o - 1, k, p],
            recv_sem=xrecv.at[o - 1, k, p],
            device_id={"tensor": lax.rem(ti + o, nt)},
            device_id_type=MESH,
        )

    def beside(u, k):
        return pltpu.make_async_remote_copy(
            src_ref=act_ref.at[k],
            dst_ref=held(k, my_col),
            send_sem=bsend.at[u - 1, k],
            recv_sem=brecv.at[u - 1, k],
            device_id={"sub": lax.rem(si + u, ns)},
            device_id_type=MESH,
        )

    def forward(u, o, k, p):
        col = lax.rem(ti + nt - o, nt) * ns + si
        return pltpu.make_async_remote_copy(
            src_ref=held(k, col, p),
            dst_ref=held(k, col, p),
            send_sem=fsend.at[u - 1, o - 1, k, p],
            recv_sem=frecv.at[u - 1, o - 1, k, p],
            device_id={"sub": lax.rem(si + u, ns)},
            device_id_type=MESH,
        )

    for k in range(CHUNKS):
        for p in range(PIECES):
            for o in range(1, nt):
                across(o, k, p).start()
    for k in range(CHUNKS):
        for u in range(1, ns):
            beside(u, k).start()

    def arrive(k):
        for p in range(PIECES):
            for o in range(1, nt):
                across(o, k, p).wait_recv()
                for u in range(1, ns):
                    forward(u, o, k, p).start()
        own_copies[k].wait()
        for u in range(1, ns):
            beside(u, k).wait_recv()
        for p in range(PIECES):
            for o in range(1, nt):
                for u in range(1, ns):
                    forward(u, o, k, p).wait_recv()

    def product(slot, k):
        left = gath[k][code_ref[0, slot]]
        right = cotv[code_ref[1, slot], k * depth:(k + 1) * depth, :]
        return lax.dot_general(left, right, (((1,), (0,)), ((), ())), preferred_element_type=jnp.float32)

    arrive(0)

    def loaded(i, carry):
        stripe(i).wait()
        return carry

    lax.fori_loop(0, stripes, loaded, 0)

    def first(i, carry):
        for j in range(UNROLL):
            slot = i * UNROLL + j
            value = product(slot, 0)
            acc[slot, 0] = value[:HALF]
            acc[slot, 1] = value[HALF:]
        return carry

    lax.fori_loop(0, slots // UNROLL, first, 0)
    arrive(1)

    lane = lax.broadcasted_iota(jnp.int32, (HALF, LANES), 1) // BS

    def finish(dev, j):
        slot = dev * pair + j
        odd = code_ref[2, slot]
        value = product(slot, 1)
        acc[slot, 0] += value[:HALF]
        acc[slot, 1] += value[HALF:]
        straight = acc[slot, odd]
        turned = acc[slot, code_ref[3, slot]]
        tile = jnp.where(lane == odd, straight, pltpu.roll(turned, BS, 1))
        top = jnp.maximum(jnp.max(jnp.abs(tile), axis=0, keepdims=True), 1e-30)
        coded = jnp.round(tile * (QMAX / top)).astype(jnp.int32).astype(jnp.int16)
        sendq[dev, j] = coded
        sendc[dev, j] = top * (live_ref[slot] * (1.0 / QMAX))

    def tiles_to(dev):
        return pltpu.make_async_remote_copy(
            src_ref=sendq.at[dev], dst_ref=recvq.at[me],
            send_sem=qsend.at[dev], recv_sem=qrecv.at[me],
            device_id=at(dev), device_id_type=MESH,
        )

    def scales_to(dev):
        return pltpu.make_async_remote_copy(
            src_ref=sendc.at[dev], dst_ref=recvc.at[me],
            send_sem=csend.at[dev], recv_sem=crecv.at[me],
            device_id=at(dev), device_id_type=MESH,
        )

    def tiles_from(dev):
        return pltpu.make_async_remote_copy(
            src_ref=sendq.at[dev], dst_ref=recvq.at[dev],
            send_sem=qsend.at[dev], recv_sem=qrecv.at[dev],
            device_id=at(dev), device_id_type=MESH,
        )

    def scales_from(dev):
        return pltpu.make_async_remote_copy(
            src_ref=sendc.at[dev], dst_ref=recvc.at[dev],
            send_sem=csend.at[dev], recv_sem=crecv.at[dev],
            device_id=at(dev), device_id_type=MESH,
        )

    def partner(i):
        hop = ndp - 1 - i // ncol
        col = lax.rem(my_col + ncol - 1 - lax.rem(i, ncol), ncol)
        return lax.rem(dp + hop, ndp) * ncol + col

    def second(i, carry):
        dev = partner(i)
        for j in range(pair):
            finish(dev, j)

        @pl.when(i < owners - 1)
        def _():
            tiles_to(dev).start()
            scales_to(dev).start()

        return carry

    lax.fori_loop(0, owners, second, 0)
    own_tiles = pltpu.make_async_copy(sendq.at[me], recvq.at[me], local_sem.at[0])
    own_scales = pltpu.make_async_copy(sendc.at[me], recvc.at[me], local_sem.at[1])
    own_tiles.start()
    own_scales.start()

    def collect(i, carry):
        dev = partner(i)
        tiles_from(dev).wait_recv()
        scales_from(dev).wait_recv()
        return carry

    lax.fori_loop(0, owners - 1, collect, 0)
    own_tiles.wait()
    own_scales.wait()

    here = lax.broadcasted_iota(jnp.int32, (HALF // 2, LANES), 1) < BS
    group = min(4, out_ref.shape[0])

    def settle(i, carry):
        for b in range(group):
            j = i * group + b
            col = src_ref[0, j]
            rank = src_ref[1, j]
            value = None
            for d in range(ndp):
                source = d * ncol + col
                part = recvq[source, rank].astype(jnp.int32).astype(jnp.float32)
                part = part * recvc[source, rank]
                value = part if value is None else value + part
            total[b] = value
            even = total[b, pl.ds(0, HALF // 2, stride=2), :]
            odd = total[b, pl.ds(1, HALF // 2, stride=2), :]
            out_ref[j, :HALF // 2, :] = jnp.where(here, even, pltpu.roll(odd, BS, 1))
            out_ref[j, HALF // 2:, :] = jnp.where(here, pltpu.roll(even, BS, 1), odd)
        return carry

    lax.fori_loop(0, out_ref.shape[0] // group, settle, 0)

    for k in range(CHUNKS):
        for u in range(1, ns):
            beside(u, k).wait_send()
        for p in range(PIECES):
            for o in range(1, nt):
                across(o, k, p).wait_send()
                for u in range(1, ns):
                    forward(u, o, k, p).wait_send()

    def sent(i, carry):
        dev = partner(i)
        tiles_to(dev).wait_send()
        scales_to(dev).wait_send()
        return carry

    lax.fori_loop(0, owners - 1, sent, 0)


def local(ndp, nt, ns, activations, cotangents, block_rows, block_cols, live_counts, owner_device, owner_slot):
    ncol = nt * ns
    owners = ndp * ncol
    tokens, feats = activations.shape
    slots = block_rows.shape[1]
    cap = slots // ndp
    pair = slots // owners
    depth = tokens // CHUNKS
    my_col = lax.axis_index(("tensor", "sub"))
    me = lax.axis_index("dp") * ncol + my_col

    keys = owner_device * cap + owner_slot
    key = lax.dynamic_index_in_dim(keys, my_col, 0, keepdims=False)
    position = jnp.sum((key[None, :] < key[:, None]).astype(jnp.int32), axis=1)
    match = position[None, :] == jnp.arange(slots, dtype=jnp.int32)[:, None]
    order = jnp.sum(jnp.where(match, block_rows * 1024 + block_cols, 0), axis=1)
    odd = order % 2
    codes = jnp.stack([order // 1024, order % 1024 // 2, odd, 1 - odd])
    alive = jnp.arange(slots, dtype=jnp.int32)[None, :] < live_counts[0]
    live = jnp.sum(jnp.where(match & alive, 1.0, 0.0), axis=1)

    mine = owner_device == me
    lower = owner_slot[:, None, :] < owner_slot[:, :, None]
    rank = jnp.sum((lower & mine[:, None, :]).astype(jnp.int32), axis=2)
    where_from = jnp.arange(ncol, dtype=jnp.int32)[:, None] * pair + rank
    here = mine[None] & (owner_slot[None] == jnp.arange(cap, dtype=jnp.int32)[:, None, None])
    source = jnp.sum(jnp.where(here, where_from[None], 0), axis=(1, 2))
    sources = jnp.stack([source // pair, source % pair])

    turned = activations.reshape(CHUNKS, depth, feats).transpose(0, 2, 1).reshape(CHUNKS, feats // BS, BS, depth)

    dma = pltpu.SemaphoreType.DMA
    result = pl.pallas_call(
        functools.partial(kernel, ndp, nt, ns),
        out_shape=jax.ShapeDtypeStruct((cap, HALF, LANES), jnp.float32),
        in_specs=[
            pl.BlockSpec(memory_space=pltpu.SMEM),
            pl.BlockSpec(memory_space=pltpu.SMEM),
            pl.BlockSpec(memory_space=pltpu.SMEM),
            pl.BlockSpec(memory_space=pl.ANY),
            pl.BlockSpec(memory_space=pl.ANY),
        ],
        out_specs=pl.BlockSpec(memory_space=pltpu.VMEM),
        scratch_shapes=[
            pltpu.VMEM((ncol * feats // BS, BS, depth), jnp.bfloat16),
            pltpu.VMEM((ncol * feats // BS, BS, depth), jnp.bfloat16),
            pltpu.VMEM((cotangents.shape[1] // LANES, tokens, LANES), jnp.bfloat16),
            pltpu.VMEM((slots, 2, HALF, LANES), jnp.float32),
            pltpu.VMEM((owners, pair, HALF, LANES), jnp.int16),
            pltpu.VMEM((owners, pair, 1, LANES), jnp.float32),
            pltpu.VMEM((owners, pair, HALF, LANES), jnp.int16),
            pltpu.VMEM((owners, pair, 1, LANES), jnp.float32),
            pltpu.VMEM((4, HALF, LANES), jnp.float32),
            dma((cotangents.shape[1] // LANES,)),
            dma((1 + CHUNKS,)),
            dma((ns - 1, CHUNKS)),
            dma((ns - 1, CHUNKS)),
            dma((nt - 1, CHUNKS, PIECES)),
            dma((nt - 1, CHUNKS, PIECES)),
            dma((ns - 1, nt - 1, CHUNKS, PIECES)),
            dma((ns - 1, nt - 1, CHUNKS, PIECES)),
            dma((owners,)),
            dma((owners,)),
            dma((owners,)),
            dma((owners,)),
        ],
        compiler_params=pltpu.CompilerParams(
            collective_id=0, has_side_effects=True, vmem_limit_bytes=52 * 1024 * 1024
        ),
        cost_estimate=pl.CostEstimate(flops=2 * slots * tokens * BS * LANES, bytes_accessed=16 << 20, transcendentals=0),
    )(codes, live, sources, turned, cotangents)
    return result.reshape(1, cap, BS * BS)


def solution(mesh):
    placed = (
        P(("groups", "dp"), ("tensor", "sub")),
        P(("groups", "dp"), ("tensor", "sub")),
        P(("tensor", "sub"), None),
        P(("tensor", "sub"), None),
        P(("tensor", "sub")),
        P(),
        P(),
    )
    return jax.shard_map(
        functools.partial(local, mesh.shape["dp"], mesh.shape["tensor"], mesh.shape["sub"]),
        mesh=mesh,
        in_specs=placed,
        out_specs=P(("groups", "dp", "tensor", "sub"), None, None),
        check_vma=False,
    )
```

```python
import functools

import jax
import jax.numpy as jnp
from jax import lax
from jax.experimental import pallas as pl
from jax.experimental.pallas import tpu as pltpu
from jax.sharding import PartitionSpec as P

BS = 64
HALF = 32
LANES = 128
QMAX = 32767.0
CHUNKS = 2
PIECES = 4
UNROLL = 8
MESH = pl.DeviceIdType.MESH


def kernel(
    ndp, nt, ns,
    code_ref, live_ref, src_ref, act_ref, cot_ref,
    out_ref,
    early, late, cotv, acc, sendq, sendc, relayq, relayc, recvq, recvc, total,
    cot_sem, local_sem, bsend, brecv, xsend, xrecv, fsend, frecv,
    qsend, csend, rqrecv, rcrecv, qrecv, crecv,
):
    ncol = nt * ns
    dp = lax.axis_index("dp")
    ti = lax.axis_index("tensor")
    si = lax.axis_index("sub")
    my_col = ti * ns + si
    me = dp * ncol + my_col
    owners = ndp * ncol
    feats = act_ref.shape[1]
    depth = act_ref.shape[3]
    piece = feats // PIECES
    stripes = cotv.shape[0]
    slots = acc.shape[0]
    gath = (early, late)
    pair = slots // owners

    def at(dev):
        return {"dp": dev // ncol, "tensor": lax.rem(dev, ncol) // ns, "sub": lax.rem(dev, ns)}

    def held(k, col, p=None):
        if p is None:
            return gath[k].at[pl.ds(col * feats, feats)]
        return gath[k].at[pl.ds(col * feats + p * piece, piece)]

    def stripe(i):
        return pltpu.make_async_copy(
            cot_ref.at[:, pl.ds(pl.multiple_of(i * LANES, LANES), LANES)], cotv.at[i], cot_sem.at[i]
        )

    def load(i, carry):
        stripe(i).start()
        return carry

    lax.fori_loop(0, stripes, load, 0)
    own_copies = [
        pltpu.make_async_copy(act_ref.at[k], held(k, my_col), local_sem.at[1 + k]) for k in range(CHUNKS)
    ]
    for copy in own_copies:
        copy.start()

    relayc[...] = jnp.zeros_like(relayc)
    recvc[...] = jnp.zeros_like(recvc)

    barrier = pltpu.get_barrier_semaphore()

    def greet(i, carry):
        z = dp + i // ncol - 1
        dev = z * ncol + lax.rem(i, ncol)

        @pl.when((z >= 0) & (z < ndp) & (dev != me))
        def _():
            pl.semaphore_signal(barrier, inc=1, device_id=at(dev), device_id_type=MESH)

        return carry

    lax.fori_loop(0, 3 * ncol, greet, 0)
    at_end = (dp == 0) | (dp == ndp - 1)

    @pl.when(at_end)
    def _():
        pl.semaphore_wait(barrier, 2 * ncol - 1)

    @pl.when(jnp.logical_not(at_end))
    def _():
        pl.semaphore_wait(barrier, 3 * ncol - 1)

    def across(o, k, p):
        return pltpu.make_async_remote_copy(
            src_ref=act_ref.at[k, pl.ds(p * piece, piece)],
            dst_ref=held(k, my_col, p),
            send_sem=xsend.at[o - 1, k, p],
            recv_sem=xrecv.at[o - 1, k, p],
            device_id={"tensor": lax.rem(ti + o, nt)},
            device_id_type=MESH,
        )

    def beside(u, k):
        return pltpu.make_async_remote_copy(
            src_ref=act_ref.at[k],
            dst_ref=held(k, my_col),
            send_sem=bsend.at[u - 1, k],
            recv_sem=brecv.at[u - 1, k],
            device_id={"sub": lax.rem(si + u, ns)},
            device_id_type=MESH,
        )

    def forward(u, o, k, p):
        col = lax.rem(ti + nt - o, nt) * ns + si
        return pltpu.make_async_remote_copy(
            src_ref=held(k, col, p),
            dst_ref=held(k, col, p),
            send_sem=fsend.at[u - 1, o - 1, k, p],
            recv_sem=frecv.at[u - 1, o - 1, k, p],
            device_id={"sub": lax.rem(si + u, ns)},
            device_id_type=MESH,
        )

    for k in range(CHUNKS):
        for p in range(PIECES):
            for o in range(1, nt):
                across(o, k, p).start()
    for k in range(CHUNKS):
        for u in range(1, ns):
            beside(u, k).start()

    def arrive(k):
        for p in range(PIECES):
            for o in range(1, nt):
                across(o, k, p).wait_recv()
                for u in range(1, ns):
                    forward(u, o, k, p).start()
        own_copies[k].wait()
        for u in range(1, ns):
            beside(u, k).wait_recv()
        for p in range(PIECES):
            for o in range(1, nt):
                for u in range(1, ns):
                    forward(u, o, k, p).wait_recv()

    def product(slot, k):
        left = gath[k][code_ref[0, slot]]
        right = cotv[code_ref[1, slot], k * depth:(k + 1) * depth, :]
        return lax.dot_general(left, right, (((1,), (0,)), ((), ())), preferred_element_type=jnp.float32)

    arrive(0)

    def loaded(i, carry):
        stripe(i).wait()
        return carry

    lax.fori_loop(0, stripes, loaded, 0)

    def first(i, carry):
        for j in range(UNROLL):
            slot = i * UNROLL + j
            value = product(slot, 0)
            acc[slot, 0] = value[:HALF]
            acc[slot, 1] = value[HALF:]
        return carry

    lax.fori_loop(0, slots // UNROLL, first, 0)
    arrive(1)

    lane = lax.broadcasted_iota(jnp.int32, (HALF, LANES), 1) // BS

    def finish(dev, j):
        slot = dev * pair + j
        odd = code_ref[2, slot]
        value = product(slot, 1)
        acc[slot, 0] += value[:HALF]
        acc[slot, 1] += value[HALF:]
        straight = acc[slot, odd]
        turned = acc[slot, code_ref[3, slot]]
        tile = jnp.where(lane == odd, straight, pltpu.roll(turned, BS, 1))
        tile += relayq[dev, j].astype(jnp.int32).astype(jnp.float32) * relayc[dev, j]
        top = jnp.maximum(jnp.max(jnp.abs(tile), axis=0, keepdims=True), 1e-30)
        coded = jnp.round(tile * (QMAX / top)).astype(jnp.int32).astype(jnp.int16)
        sendq[dev, j] = coded
        sendc[dev, j] = top * (live_ref[slot] * (1.0 / QMAX))

    def send(src, dst, send_sem, recv_sem, dev):
        return pltpu.make_async_remote_copy(
            src_ref=src, dst_ref=dst, send_sem=send_sem, recv_sem=recv_sem,
            device_id=at(dev), device_id_type=MESH,
        )

    def relayed(dev, to):
        return (
            send(sendq.at[dev], relayq.at[dev], qsend.at[dev], rqrecv.at[dev], to),
            send(sendc.at[dev], relayc.at[dev], csend.at[dev], rcrecv.at[dev], to),
        )

    def delivered(dev, flow, col, to):
        return (
            send(sendq.at[dev], recvq.at[flow, col], qsend.at[dev], qrecv.at[flow, col], to),
            send(sendc.at[dev], recvc.at[flow, col], csend.at[dev], crecv.at[flow, col], to),
        )

    own_tiles = pltpu.make_async_copy(sendq.at[me], recvq.at[2, my_col], local_sem.at[1])
    own_scales = pltpu.make_async_copy(sendc.at[me], recvc.at[2, my_col], local_sem.at[2])

    upper = 2 * dp // ndp

    def step(i, carry):
        per = 3 * ncol
        ring = i // per
        col = lax.rem(my_col + 1 + lax.rem(i, ncol), ncol)
        turn = lax.rem(i, per) // ncol
        flow = turn + upper * (1 - 2 * turn) * (2 - turn) * (turn + 1) // 2
        up = (1 - flow) * (2 - flow) // 2
        down = flow * (2 - flow)
        own = flow * (flow - 1) // 2
        goal = up * (ndp - 1 - ring) + down * ring + own * dp
        way = up - down
        dev = goal * ncol + col
        far = (goal - dp) * way

        @pl.when(far + own * (1 - ring) > 0)
        def _():
            @pl.when(up * dp + down * (ndp - 1 - dp) > 0)
            def _():
                for copy in relayed(dev, lax.rem(me + ncol, owners)):
                    copy.wait_recv()

            for j in range(pair):
                finish(dev, j)

            @pl.when(far > 1)
            def _():
                for copy in relayed(dev, (dp + way) * ncol + my_col):
                    copy.start()

            @pl.when((far < 2) & (dev != me))
            def _():
                for copy in delivered(dev, flow, my_col, dev):
                    copy.start()

            @pl.when(dev == me)
            def _():
                own_tiles.start()
                own_scales.start()

        return carry

    lax.fori_loop(0, (ndp - 1) * 3 * ncol, step, 0)

    def collect(i, carry):
        flow = i // ncol
        col = lax.rem(i, ncol)

        @pl.when(((flow == 0) & (dp > 0)) | ((flow == 1) & (dp < ndp - 1)) | ((flow == 2) & (col != my_col)))
        def _():
            for copy in delivered(me, flow, col, lax.rem(me + ncol, owners)):
                copy.wait_recv()

        return carry

    lax.fori_loop(0, 3 * ncol, collect, 0)
    own_tiles.wait()
    own_scales.wait()

    here = lax.broadcasted_iota(jnp.int32, (HALF // 2, LANES), 1) < BS
    group = min(4, out_ref.shape[0])

    def settle(i, carry):
        for b in range(group):
            j = i * group + b
            col = src_ref[0, j]
            rank = src_ref[1, j]
            value = None
            for flow in range(3):
                part = recvq[flow, col, rank].astype(jnp.int32).astype(jnp.float32)
                part = part * recvc[flow, col, rank]
                value = part if value is None else value + part
            total[b] = value
            even = total[b, pl.ds(0, HALF // 2, stride=2), :]
            odd = total[b, pl.ds(1, HALF // 2, stride=2), :]
            out_ref[j, :HALF // 2, :] = jnp.where(here, even, pltpu.roll(odd, BS, 1))
            out_ref[j, HALF // 2:, :] = jnp.where(here, pltpu.roll(even, BS, 1), odd)
        return carry

    lax.fori_loop(0, out_ref.shape[0] // group, settle, 0)

    for k in range(CHUNKS):
        for u in range(1, ns):
            beside(u, k).wait_send()
        for p in range(PIECES):
            for o in range(1, nt):
                across(o, k, p).wait_send()
                for u in range(1, ns):
                    forward(u, o, k, p).wait_send()

    def sent(i, carry):
        dev = lax.rem(me + i, owners)
        for copy in relayed(dev, dev):
            copy.wait_send()
        return carry

    lax.fori_loop(1, owners, sent, 0)


def local(ndp, nt, ns, activations, cotangents, block_rows, block_cols, live_counts, owner_device, owner_slot):
    ncol = nt * ns
    owners = ndp * ncol
    tokens, feats = activations.shape
    slots = block_rows.shape[1]
    cap = slots // ndp
    pair = slots // owners
    depth = tokens // CHUNKS
    my_col = lax.axis_index(("tensor", "sub"))
    me = lax.axis_index("dp") * ncol + my_col

    keys = owner_device * cap + owner_slot
    key = lax.dynamic_index_in_dim(keys, my_col, 0, keepdims=False)
    position = jnp.sum((key[None, :] < key[:, None]).astype(jnp.int32), axis=1)
    match = position[None, :] == jnp.arange(slots, dtype=jnp.int32)[:, None]
    order = jnp.sum(jnp.where(match, block_rows * 1024 + block_cols, 0), axis=1)
    odd = order % 2
    codes = jnp.stack([order // 1024, order % 1024 // 2, odd, 1 - odd])
    alive = jnp.arange(slots, dtype=jnp.int32)[None, :] < live_counts[0]
    live = jnp.sum(jnp.where(match & alive, 1.0, 0.0), axis=1)

    mine = owner_device == me
    lower = owner_slot[:, None, :] < owner_slot[:, :, None]
    rank = jnp.sum((lower & mine[:, None, :]).astype(jnp.int32), axis=2)
    where_from = jnp.arange(ncol, dtype=jnp.int32)[:, None] * pair + rank
    here = mine[None] & (owner_slot[None] == jnp.arange(cap, dtype=jnp.int32)[:, None, None])
    source = jnp.sum(jnp.where(here, where_from[None], 0), axis=(1, 2))
    sources = jnp.stack([source // pair, source % pair])

    turned = activations.reshape(CHUNKS, depth, feats).transpose(0, 2, 1).reshape(CHUNKS, feats // BS, BS, depth)

    dma = pltpu.SemaphoreType.DMA
    result = pl.pallas_call(
        functools.partial(kernel, ndp, nt, ns),
        out_shape=jax.ShapeDtypeStruct((cap, HALF, LANES), jnp.float32),
        in_specs=[
            pl.BlockSpec(memory_space=pltpu.SMEM),
            pl.BlockSpec(memory_space=pltpu.SMEM),
            pl.BlockSpec(memory_space=pltpu.SMEM),
            pl.BlockSpec(memory_space=pl.ANY),
            pl.BlockSpec(memory_space=pl.ANY),
        ],
        out_specs=pl.BlockSpec(memory_space=pltpu.VMEM),
        scratch_shapes=[
            pltpu.VMEM((ncol * feats // BS, BS, depth), jnp.bfloat16),
            pltpu.VMEM((ncol * feats // BS, BS, depth), jnp.bfloat16),
            pltpu.VMEM((cotangents.shape[1] // LANES, tokens, LANES), jnp.bfloat16),
            pltpu.VMEM((slots, 2, HALF, LANES), jnp.float32),
            pltpu.VMEM((owners, pair, HALF, LANES), jnp.int16),
            pltpu.VMEM((owners, pair, 1, LANES), jnp.float32),
            pltpu.VMEM((owners, pair, HALF, LANES), jnp.int16),
            pltpu.VMEM((owners, pair, 1, LANES), jnp.float32),
            pltpu.VMEM((3, ncol, pair, HALF, LANES), jnp.int16),
            pltpu.VMEM((3, ncol, pair, 1, LANES), jnp.float32),
            pltpu.VMEM((4, HALF, LANES), jnp.float32),
            dma((cotangents.shape[1] // LANES,)),
            dma((1 + CHUNKS,)),
            dma((ns - 1, CHUNKS)),
            dma((ns - 1, CHUNKS)),
            dma((nt - 1, CHUNKS, PIECES)),
            dma((nt - 1, CHUNKS, PIECES)),
            dma((ns - 1, nt - 1, CHUNKS, PIECES)),
            dma((ns - 1, nt - 1, CHUNKS, PIECES)),
            dma((owners,)),
            dma((owners,)),
            dma((owners,)),
            dma((owners,)),
            dma((3, ncol)),
            dma((3, ncol)),
        ],
        compiler_params=pltpu.CompilerParams(
            collective_id=0, has_side_effects=True, vmem_limit_bytes=52 * 1024 * 1024
        ),
        cost_estimate=pl.CostEstimate(flops=2 * slots * tokens * BS * LANES, bytes_accessed=16 << 20, transcendentals=0),
    )(codes, live, sources, turned, cotangents)
    return result.reshape(1, cap, BS * BS)


def solution(mesh):
    placed = (
        P(("groups", "dp"), ("tensor", "sub")),
        P(("groups", "dp"), ("tensor", "sub")),
        P(("tensor", "sub"), None),
        P(("tensor", "sub"), None),
        P(("tensor", "sub")),
        P(),
        P(),
    )
    return jax.shard_map(
        functools.partial(local, mesh.shape["dp"], mesh.shape["tensor"], mesh.shape["sub"]),
        mesh=mesh,
        in_specs=placed,
        out_specs=P(("groups", "dp", "tensor", "sub"), None, None),
        check_vma=False,
    )
```

```python
import functools

import jax
import jax.numpy as jnp
from jax import lax
from jax.experimental import pallas as pl
from jax.experimental.pallas import tpu as pltpu
from jax.sharding import PartitionSpec as P

BS = 64
HALF = 32
LANES = 128
QMAX = 32767.0
CHUNKS = 2
PIECES = 4
UNROLL = 8
MESH = pl.DeviceIdType.MESH


def kernel(
    ndp, nt, ns,
    code_ref, live_ref, src_ref, act_ref, cot_ref,
    out_ref,
    actv, early, late, cotv, acc, sendq, sendc, relayq, relayc, recvq, recvc, total,
    cot_sem, local_sem, bsend, brecv, xsend, xrecv, fsend, frecv,
    qsend, csend, rqrecv, rcrecv, qrecv, crecv,
):
    ncol = nt * ns
    dp = lax.axis_index("dp")
    ti = lax.axis_index("tensor")
    si = lax.axis_index("sub")
    my_col = ti * ns + si
    me = dp * ncol + my_col
    owners = ndp * ncol
    feats = act_ref.shape[1] // BS
    depth = act_ref.shape[0] // CHUNKS
    piece = feats // PIECES
    stripes = cotv.shape[0]
    slots = acc.shape[0]
    gath = (early, late)
    pair = slots // owners

    def at(dev):
        return {"dp": dev // ncol, "tensor": lax.rem(dev, ncol) // ns, "sub": lax.rem(dev, ns)}

    def held(k, col, p=None):
        if p is None:
            return gath[k].at[pl.ds(col * feats, feats)]
        return gath[k].at[pl.ds(col * feats + p * piece, piece)]

    def stripe(i):
        return pltpu.make_async_copy(
            cot_ref.at[:, pl.ds(pl.multiple_of(i * LANES, LANES), LANES)], cotv.at[i], cot_sem.at[i]
        )

    def load(i, carry):
        stripe(i).start()
        return carry

    act_copy = pltpu.make_async_copy(act_ref, actv, local_sem.at[0])
    act_copy.start()
    lax.fori_loop(0, stripes, load, 0)

    relayc[...] = jnp.zeros_like(relayc)
    recvc[...] = jnp.zeros_like(recvc)

    barrier = pltpu.get_barrier_semaphore()

    def greet(i, carry):
        z = dp + i // ncol - 1
        dev = z * ncol + lax.rem(i, ncol)

        @pl.when((z >= 0) & (z < ndp) & (dev != me))
        def _():
            pl.semaphore_signal(barrier, inc=1, device_id=at(dev), device_id_type=MESH)

        return carry

    lax.fori_loop(0, 3 * ncol, greet, 0)
    act_copy.wait()
    at_end = (dp == 0) | (dp == ndp - 1)

    @pl.when(at_end)
    def _():
        pl.semaphore_wait(barrier, 2 * ncol - 1)

    @pl.when(jnp.logical_not(at_end))
    def _():
        pl.semaphore_wait(barrier, 3 * ncol - 1)

    def across(o, k, p):
        return pltpu.make_async_remote_copy(
            src_ref=held(k, my_col, p),
            dst_ref=held(k, my_col, p),
            send_sem=xsend.at[o - 1, k, p],
            recv_sem=xrecv.at[o - 1, k, p],
            device_id={"tensor": lax.rem(ti + o, nt)},
            device_id_type=MESH,
        )

    def beside(u, k):
        return pltpu.make_async_remote_copy(
            src_ref=held(k, my_col),
            dst_ref=held(k, my_col),
            send_sem=bsend.at[u - 1, k],
            recv_sem=brecv.at[u - 1, k],
            device_id={"sub": lax.rem(si + u, ns)},
            device_id_type=MESH,
        )

    def forward(u, o, k, p):
        col = lax.rem(ti + nt - o, nt) * ns + si
        return pltpu.make_async_remote_copy(
            src_ref=held(k, col, p),
            dst_ref=held(k, col, p),
            send_sem=fsend.at[u - 1, o - 1, k, p],
            recv_sem=frecv.at[u - 1, o - 1, k, p],
            device_id={"sub": lax.rem(si + u, ns)},
            device_id_type=MESH,
        )

    for k in range(CHUNKS):
        for p in range(PIECES):
            block = actv[k * depth:(k + 1) * depth, p * piece * BS:(p + 1) * piece * BS]
            gath[k][pl.ds(my_col * feats + p * piece, piece)] = block.T.reshape(piece, BS, depth)
            for o in range(1, nt):
                across(o, k, p).start()
        for u in range(1, ns):
            beside(u, k).start()

    def arrive(k):
        for p in range(PIECES):
            for o in range(1, nt):
                across(o, k, p).wait_recv()
                for u in range(1, ns):
                    forward(u, o, k, p).start()
        for u in range(1, ns):
            beside(u, k).wait_recv()
        for p in range(PIECES):
            for o in range(1, nt):
                for u in range(1, ns):
                    forward(u, o, k, p).wait_recv()

    def product(slot, k):
        left = gath[k][code_ref[0, slot]]
        right = cotv[code_ref[1, slot], k * depth:(k + 1) * depth, :]
        return lax.dot_general(left, right, (((1,), (0,)), ((), ())), preferred_element_type=jnp.float32)

    arrive(0)

    def loaded(i, carry):
        stripe(i).wait()
        return carry

    lax.fori_loop(0, stripes, loaded, 0)

    def first(i, carry):
        for j in range(UNROLL):
            slot = i * UNROLL + j
            value = product(slot, 0)
            acc[slot, 0] = value[:HALF]
            acc[slot, 1] = value[HALF:]
        return carry

    lax.fori_loop(0, slots // UNROLL, first, 0)
    arrive(1)

    lane = lax.broadcasted_iota(jnp.int32, (HALF, LANES), 1) // BS

    def finish(dev, j):
        slot = dev * pair + j
        odd = code_ref[2, slot]
        value = product(slot, 1)
        acc[slot, 0] += value[:HALF]
        acc[slot, 1] += value[HALF:]
        straight = acc[slot, odd]
        turned = acc[slot, code_ref[3, slot]]
        tile = jnp.where(lane == odd, straight, pltpu.roll(turned, BS, 1))
        tile += relayq[dev, j].astype(jnp.int32).astype(jnp.float32) * relayc[dev, j]
        top = jnp.maximum(jnp.max(jnp.abs(tile), axis=0, keepdims=True), 1e-30)
        coded = jnp.round(tile * (QMAX / top)).astype(jnp.int32).astype(jnp.int16)
        sendq[dev, j] = coded
        sendc[dev, j] = top * (live_ref[slot] * (1.0 / QMAX))

    def send(src, dst, send_sem, recv_sem, dev):
        return pltpu.make_async_remote_copy(
            src_ref=src, dst_ref=dst, send_sem=send_sem, recv_sem=recv_sem,
            device_id=at(dev), device_id_type=MESH,
        )

    def relayed(dev, to):
        return (
            send(sendq.at[dev], relayq.at[dev], qsend.at[dev], rqrecv.at[dev], to),
            send(sendc.at[dev], relayc.at[dev], csend.at[dev], rcrecv.at[dev], to),
        )

    def delivered(dev, flow, col, to):
        return (
            send(sendq.at[dev], recvq.at[flow, col], qsend.at[dev], qrecv.at[flow, col], to),
            send(sendc.at[dev], recvc.at[flow, col], csend.at[dev], crecv.at[flow, col], to),
        )

    own_tiles = pltpu.make_async_copy(sendq.at[me], recvq.at[2, my_col], local_sem.at[1])
    own_scales = pltpu.make_async_copy(sendc.at[me], recvc.at[2, my_col], local_sem.at[2])

    upper = 2 * dp // ndp

    def step(i, carry):
        per = 3 * ncol
        ring = i // per
        col = lax.rem(my_col + 1 + lax.rem(i, ncol), ncol)
        turn = lax.rem(i, per) // ncol
        flow = turn + upper * (1 - 2 * turn) * (2 - turn) * (turn + 1) // 2
        up = (1 - flow) * (2 - flow) // 2
        down = flow * (2 - flow)
        own = flow * (flow - 1) // 2
        goal = up * (ndp - 1 - ring) + down * ring + own * dp
        way = up - down
        dev = goal * ncol + col
        far = (goal - dp) * way

        @pl.when(far + own * (1 - ring) > 0)
        def _():
            @pl.when(up * dp + down * (ndp - 1 - dp) > 0)
            def _():
                for copy in relayed(dev, lax.rem(me + ncol, owners)):
                    copy.wait_recv()

            for j in range(pair):
                finish(dev, j)

            @pl.when(far > 1)
            def _():
                for copy in relayed(dev, (dp + way) * ncol + my_col):
                    copy.start()

            @pl.when((far < 2) & (dev != me))
            def _():
                for copy in delivered(dev, flow, my_col, dev):
                    copy.start()

            @pl.when(dev == me)
            def _():
                own_tiles.start()
                own_scales.start()

        return carry

    lax.fori_loop(0, (ndp - 1) * 3 * ncol, step, 0)

    def collect(i, carry):
        flow = i // ncol
        col = lax.rem(i, ncol)

        @pl.when(((flow == 0) & (dp > 0)) | ((flow == 1) & (dp < ndp - 1)) | ((flow == 2) & (col != my_col)))
        def _():
            for copy in delivered(me, flow, col, lax.rem(me + ncol, owners)):
                copy.wait_recv()

        return carry

    lax.fori_loop(0, 3 * ncol, collect, 0)
    own_tiles.wait()
    own_scales.wait()

    here = lax.broadcasted_iota(jnp.int32, (HALF // 2, LANES), 1) < BS
    group = min(4, out_ref.shape[0])

    def settle(i, carry):
        for b in range(group):
            j = i * group + b
            col = src_ref[0, j]
            rank = src_ref[1, j]
            value = None
            for flow in range(3):
                part = recvq[flow, col, rank].astype(jnp.int32).astype(jnp.float32)
                part = part * recvc[flow, col, rank]
                value = part if value is None else value + part
            total[b] = value
            even = total[b, pl.ds(0, HALF // 2, stride=2), :]
            odd = total[b, pl.ds(1, HALF // 2, stride=2), :]
            out_ref[j, :HALF // 2, :] = jnp.where(here, even, pltpu.roll(odd, BS, 1))
            out_ref[j, HALF // 2:, :] = jnp.where(here, pltpu.roll(even, BS, 1), odd)
        return carry

    lax.fori_loop(0, out_ref.shape[0] // group, settle, 0)

    for k in range(CHUNKS):
        for u in range(1, ns):
            beside(u, k).wait_send()
        for p in range(PIECES):
            for o in range(1, nt):
                across(o, k, p).wait_send()
                for u in range(1, ns):
                    forward(u, o, k, p).wait_send()

    def sent(i, carry):
        dev = lax.rem(me + i, owners)
        for copy in relayed(dev, dev):
            copy.wait_send()
        return carry

    lax.fori_loop(1, owners, sent, 0)


def local(ndp, nt, ns, activations, cotangents, block_rows, block_cols, live_counts, owner_device, owner_slot):
    ncol = nt * ns
    owners = ndp * ncol
    tokens, feats = activations.shape
    slots = block_rows.shape[1]
    cap = slots // ndp
    pair = slots // owners
    depth = tokens // CHUNKS
    my_col = lax.axis_index(("tensor", "sub"))
    me = lax.axis_index("dp") * ncol + my_col

    keys = owner_device * cap + owner_slot
    key = lax.dynamic_index_in_dim(keys, my_col, 0, keepdims=False)
    position = jnp.sum((key[None, :] < key[:, None]).astype(jnp.int32), axis=1)
    match = position[None, :] == jnp.arange(slots, dtype=jnp.int32)[:, None]
    order = jnp.sum(jnp.where(match, block_rows * 1024 + block_cols, 0), axis=1)
    odd = order % 2
    codes = jnp.stack([order // 1024, order % 1024 // 2, odd, 1 - odd])
    alive = jnp.arange(slots, dtype=jnp.int32)[None, :] < live_counts[0]
    live = jnp.sum(jnp.where(match & alive, 1.0, 0.0), axis=1)

    mine = owner_device == me
    lower = owner_slot[:, None, :] < owner_slot[:, :, None]
    rank = jnp.sum((lower & mine[:, None, :]).astype(jnp.int32), axis=2)
    where_from = jnp.arange(ncol, dtype=jnp.int32)[:, None] * pair + rank
    here = mine[None] & (owner_slot[None] == jnp.arange(cap, dtype=jnp.int32)[:, None, None])
    source = jnp.sum(jnp.where(here, where_from[None], 0), axis=(1, 2))
    sources = jnp.stack([source // pair, source % pair])

    dma = pltpu.SemaphoreType.DMA
    result = pl.pallas_call(
        functools.partial(kernel, ndp, nt, ns),
        out_shape=jax.ShapeDtypeStruct((cap, HALF, LANES), jnp.float32),
        in_specs=[
            pl.BlockSpec(memory_space=pltpu.SMEM),
            pl.BlockSpec(memory_space=pltpu.SMEM),
            pl.BlockSpec(memory_space=pltpu.SMEM),
            pl.BlockSpec(memory_space=pl.ANY),
            pl.BlockSpec(memory_space=pl.ANY),
        ],
        out_specs=pl.BlockSpec(memory_space=pltpu.VMEM),
        scratch_shapes=[
            pltpu.VMEM((tokens, feats), jnp.bfloat16),
            pltpu.VMEM((ncol * feats // BS, BS, depth), jnp.bfloat16),
            pltpu.VMEM((ncol * feats // BS, BS, depth), jnp.bfloat16),
            pltpu.VMEM((cotangents.shape[1] // LANES, tokens, LANES), jnp.bfloat16),
            pltpu.VMEM((slots, 2, HALF, LANES), jnp.float32),
            pltpu.VMEM((owners, pair, HALF, LANES), jnp.int16),
            pltpu.VMEM((owners, pair, 1, LANES), jnp.float32),
            pltpu.VMEM((owners, pair, HALF, LANES), jnp.int16),
            pltpu.VMEM((owners, pair, 1, LANES), jnp.float32),
            pltpu.VMEM((3, ncol, pair, HALF, LANES), jnp.int16),
            pltpu.VMEM((3, ncol, pair, 1, LANES), jnp.float32),
            pltpu.VMEM((4, HALF, LANES), jnp.float32),
            dma((cotangents.shape[1] // LANES,)),
            dma((1 + CHUNKS,)),
            dma((ns - 1, CHUNKS)),
            dma((ns - 1, CHUNKS)),
            dma((nt - 1, CHUNKS, PIECES)),
            dma((nt - 1, CHUNKS, PIECES)),
            dma((ns - 1, nt - 1, CHUNKS, PIECES)),
            dma((ns - 1, nt - 1, CHUNKS, PIECES)),
            dma((owners,)),
            dma((owners,)),
            dma((owners,)),
            dma((owners,)),
            dma((3, ncol)),
            dma((3, ncol)),
        ],
        compiler_params=pltpu.CompilerParams(
            collective_id=0, has_side_effects=True, vmem_limit_bytes=52 * 1024 * 1024
        ),
        cost_estimate=pl.CostEstimate(flops=2 * slots * tokens * BS * LANES, bytes_accessed=16 << 20, transcendentals=0),
    )(codes, live, sources, activations, cotangents)
    return result.reshape(1, cap, BS * BS)


def solution(mesh):
    placed = (
        P(("groups", "dp"), ("tensor", "sub")),
        P(("groups", "dp"), ("tensor", "sub")),
        P(("tensor", "sub"), None),
        P(("tensor", "sub"), None),
        P(("tensor", "sub")),
        P(),
        P(),
    )
    return jax.shard_map(
        functools.partial(local, mesh.shape["dp"], mesh.shape["tensor"], mesh.shape["sub"]),
        mesh=mesh,
        in_specs=placed,
        out_specs=P(("groups", "dp", "tensor", "sub"), None, None),
        check_vma=False,
    )
```

```python
import functools

import jax
import jax.numpy as jnp
from jax import lax
from jax.experimental import pallas as pl
from jax.experimental.pallas import tpu as pltpu
from jax.sharding import PartitionSpec as P

BS = 64
HALF = 32
LANES = 128
QMAX = 32767.0
CHUNKS = 2
PIECES = 4
UNROLL = 8
MESH = pl.DeviceIdType.MESH


def kernel(
    ndp, nt, ns,
    rows_ref, cols_ref, live_ref, device_ref, place_ref, act_ref, cot_ref,
    out_ref,
    code_rows, src_rows, code_ref, src_ref, actv, early, late, cotv, acc, sendq, sendc, relayq, relayc, recvq, recvc, total,
    cot_sem, table_sem, local_sem, bsend, brecv, xsend, xrecv, fsend, frecv,
    qsend, csend, rqrecv, rcrecv, qrecv, crecv,
):
    ncol = nt * ns
    dp = lax.axis_index("dp")
    ti = lax.axis_index("tensor")
    si = lax.axis_index("sub")
    my_col = ti * ns + si
    me = dp * ncol + my_col
    owners = ndp * ncol
    feats = act_ref.shape[1] // BS
    depth = act_ref.shape[0] // CHUNKS
    piece = feats // PIECES
    stripes = cotv.shape[0]
    slots = acc.shape[0]
    gath = (early, late)
    pair = slots // owners

    def at(dev):
        return {"dp": dev // ncol, "tensor": lax.rem(dev, ncol) // ns, "sub": lax.rem(dev, ns)}

    def held(k, col, p=None):
        if p is None:
            return gath[k].at[pl.ds(col * feats, feats)]
        return gath[k].at[pl.ds(col * feats + p * piece, piece)]

    def stripe(i):
        return pltpu.make_async_copy(
            cot_ref.at[:, pl.ds(pl.multiple_of(i * LANES, LANES), LANES)], cotv.at[i], cot_sem.at[i]
        )

    def load(i, carry):
        stripe(i).start()
        return carry

    act_copy = pltpu.make_async_copy(act_ref, actv, local_sem.at[0])
    act_copy.start()
    lax.fori_loop(0, stripes, load, 0)

    relayc[...] = jnp.zeros_like(relayc)
    recvc[...] = jnp.zeros_like(recvc)

    barrier = pltpu.get_barrier_semaphore()

    def greet(i, carry):
        z = dp + i // ncol - 1
        dev = z * ncol + lax.rem(i, ncol)

        @pl.when((z >= 0) & (z < ndp) & (dev != me))
        def _():
            pl.semaphore_signal(barrier, inc=1, device_id=at(dev), device_id_type=MESH)

        return carry

    lax.fori_loop(0, 3 * ncol, greet, 0)
    act_copy.wait()
    at_end = (dp == 0) | (dp == ndp - 1)

    @pl.when(at_end)
    def _():
        pl.semaphore_wait(barrier, 2 * ncol - 1)

    @pl.when(jnp.logical_not(at_end))
    def _():
        pl.semaphore_wait(barrier, 3 * ncol - 1)

    def across(o, k, p):
        return pltpu.make_async_remote_copy(
            src_ref=held(k, my_col, p),
            dst_ref=held(k, my_col, p),
            send_sem=xsend.at[o - 1, k, p],
            recv_sem=xrecv.at[o - 1, k, p],
            device_id={"tensor": lax.rem(ti + o, nt)},
            device_id_type=MESH,
        )

    def beside(u, k):
        return pltpu.make_async_remote_copy(
            src_ref=held(k, my_col),
            dst_ref=held(k, my_col),
            send_sem=bsend.at[u - 1, k],
            recv_sem=brecv.at[u - 1, k],
            device_id={"sub": lax.rem(si + u, ns)},
            device_id_type=MESH,
        )

    def forward(u, o, k, p):
        col = lax.rem(ti + nt - o, nt) * ns + si
        return pltpu.make_async_remote_copy(
            src_ref=held(k, col, p),
            dst_ref=held(k, col, p),
            send_sem=fsend.at[u - 1, o - 1, k, p],
            recv_sem=frecv.at[u - 1, o - 1, k, p],
            device_id={"sub": lax.rem(si + u, ns)},
            device_id_type=MESH,
        )

    for k in range(CHUNKS):
        for p in range(PIECES):
            block = actv[k * depth:(k + 1) * depth, p * piece * BS:(p + 1) * piece * BS]
            gath[k][pl.ds(my_col * feats + p * piece, piece)] = block.T.reshape(piece, BS, depth)
            for o in range(1, nt):
                across(o, k, p).start()
        for u in range(1, ns):
            beside(u, k).start()

    def arrive(k):
        for p in range(PIECES):
            for o in range(1, nt):
                across(o, k, p).wait_recv()
                for u in range(1, ns):
                    forward(u, o, k, p).start()
        for u in range(1, ns):
            beside(u, k).wait_recv()
        for p in range(PIECES):
            for o in range(1, nt):
                for u in range(1, ns):
                    forward(u, o, k, p).wait_recv()

    def product(slot, k):
        left = gath[k][code_ref[0, slot]]
        right = cotv[code_ref[1, slot], k * depth:(k + 1) * depth, :]
        return lax.dot_general(left, right, (((1,), (0,)), ((), ())), preferred_element_type=jnp.float32)

    cap = out_ref.shape[0]
    down_rows = lax.broadcasted_iota(jnp.int32, (slots, slots), 0)
    over_lanes = lax.broadcasted_iota(jnp.int32, (slots, slots), 1)

    def upright(row):
        return jnp.sum(jnp.where(down_rows == over_lanes, row, 0), axis=1, keepdims=True)

    key = device_ref[pl.ds(my_col, 1), :] * cap + place_ref[pl.ds(my_col, 1), :]
    position = jnp.sum(jnp.where(upright(key) < key, 1, 0), axis=0, keepdims=True)
    alive = jnp.where(over_lanes[:1] < live_ref[0], 1, 0)
    code = upright(rows_ref[...] * 1024 + cols_ref[...] * 2 + alive)
    order = jnp.sum(jnp.where(upright(position) == over_lanes, code, 0), axis=0, keepdims=True)
    odd_col = (order >> 1) & 1
    code_rows[...] = jnp.zeros_like(code_rows)
    src_rows[...] = jnp.zeros_like(src_rows)
    code_rows[0:1, :] = jnp.minimum(order >> 10, early.shape[0] - 1)
    code_rows[1:2, :] = jnp.minimum((order & 1023) >> 2, stripes - 1)
    code_rows[2:3, :] = odd_col
    code_rows[3:4, :] = 1 - odd_col
    code_rows[4:5, :] = order & 1

    places = lax.broadcasted_iota(jnp.int32, (slots, src_rows.shape[1]), 1)
    from_col = jnp.zeros((1, src_rows.shape[1]), jnp.int32)
    from_rank = jnp.zeros((1, src_rows.shape[1]), jnp.int32)
    for g in range(ncol):
        mine = upright(jnp.where(device_ref[g:g + 1, :] == me, place_ref[g:g + 1, :], 1 << 20))
        has = jnp.sum(jnp.where(mine == places, 1, 0), axis=0, keepdims=True)
        from_col += has * g
        from_rank += has * jnp.sum(jnp.where(mine < places, 1, 0), axis=0, keepdims=True)
    src_rows[0:1, :] = jnp.minimum(from_col, ncol - 1)
    src_rows[1:2, :] = jnp.minimum(from_rank, pair - 1)
    tables = (
        pltpu.make_async_copy(code_rows, code_ref, table_sem.at[0]),
        pltpu.make_async_copy(src_rows, src_ref, table_sem.at[1]),
    )
    for copy in tables:
        copy.start()
    for copy in tables:
        copy.wait()

    arrive(0)

    def loaded(i, carry):
        stripe(i).wait()
        return carry

    lax.fori_loop(0, stripes, loaded, 0)

    def first(i, carry):
        for j in range(UNROLL):
            slot = i * UNROLL + j
            value = product(slot, 0)
            acc[slot, 0] = value[:HALF]
            acc[slot, 1] = value[HALF:]
        return carry

    lax.fori_loop(0, slots // UNROLL, first, 0)
    arrive(1)

    lane = lax.broadcasted_iota(jnp.int32, (HALF, LANES), 1) // BS

    def finish(dev, j):
        slot = dev * pair + j
        odd = code_ref[2, slot]
        value = product(slot, 1)
        acc[slot, 0] += value[:HALF]
        acc[slot, 1] += value[HALF:]
        straight = acc[slot, odd]
        turned = acc[slot, code_ref[3, slot]]
        tile = jnp.where(lane == odd, straight, pltpu.roll(turned, BS, 1))
        tile += relayq[dev, j].astype(jnp.int32).astype(jnp.float32) * relayc[dev, j]
        top = jnp.maximum(jnp.max(jnp.abs(tile), axis=0, keepdims=True), 1e-30)
        coded = jnp.round(tile * (QMAX / top)).astype(jnp.int32).astype(jnp.int16)
        sendq[dev, j] = coded
        sendc[dev, j] = top * (code_ref[4, slot].astype(jnp.float32) * (1.0 / QMAX))

    def send(src, dst, send_sem, recv_sem, dev):
        return pltpu.make_async_remote_copy(
            src_ref=src, dst_ref=dst, send_sem=send_sem, recv_sem=recv_sem,
            device_id=at(dev), device_id_type=MESH,
        )

    def relayed(dev, to):
        return (
            send(sendq.at[dev], relayq.at[dev], qsend.at[dev], rqrecv.at[dev], to),
            send(sendc.at[dev], relayc.at[dev], csend.at[dev], rcrecv.at[dev], to),
        )

    def delivered(dev, flow, col, to):
        return (
            send(sendq.at[dev], recvq.at[flow, col], qsend.at[dev], qrecv.at[flow, col], to),
            send(sendc.at[dev], recvc.at[flow, col], csend.at[dev], crecv.at[flow, col], to),
        )

    own_tiles = pltpu.make_async_copy(sendq.at[me], recvq.at[2, my_col], local_sem.at[1])
    own_scales = pltpu.make_async_copy(sendc.at[me], recvc.at[2, my_col], local_sem.at[2])

    upper = 2 * dp // ndp

    def step(i, carry):
        per = 3 * ncol
        ring = i // per
        col = lax.rem(my_col + 1 + lax.rem(i, ncol), ncol)
        turn = lax.rem(i, per) // ncol
        flow = turn + upper * (1 - 2 * turn) * (2 - turn) * (turn + 1) // 2
        up = (1 - flow) * (2 - flow) // 2
        down = flow * (2 - flow)
        own = flow * (flow - 1) // 2
        goal = up * (ndp - 1 - ring) + down * ring + own * dp
        way = up - down
        dev = goal * ncol + col
        far = (goal - dp) * way

        @pl.when(far + own * (1 - ring) > 0)
        def _():
            @pl.when(up * dp + down * (ndp - 1 - dp) > 0)
            def _():
                for copy in relayed(dev, lax.rem(me + ncol, owners)):
                    copy.wait_recv()

            for j in range(pair):
                finish(dev, j)

            @pl.when(far > 1)
            def _():
                for copy in relayed(dev, (dp + way) * ncol + my_col):
                    copy.start()

            @pl.when((far < 2) & (dev != me))
            def _():
                for copy in delivered(dev, flow, my_col, dev):
                    copy.start()

            @pl.when(dev == me)
            def _():
                own_tiles.start()
                own_scales.start()

        return carry

    lax.fori_loop(0, (ndp - 1) * 3 * ncol, step, 0)

    def collect(i, carry):
        flow = i // ncol
        col = lax.rem(i, ncol)

        @pl.when(((flow == 0) & (dp > 0)) | ((flow == 1) & (dp < ndp - 1)) | ((flow == 2) & (col != my_col)))
        def _():
            for copy in delivered(me, flow, col, lax.rem(me + ncol, owners)):
                copy.wait_recv()

        return carry

    lax.fori_loop(0, 3 * ncol, collect, 0)
    own_tiles.wait()
    own_scales.wait()

    here = lax.broadcasted_iota(jnp.int32, (HALF // 2, LANES), 1) < BS
    group = min(4, out_ref.shape[0])

    def settle(i, carry):
        for b in range(group):
            j = i * group + b
            col = src_ref[0, j]
            rank = src_ref[1, j]
            value = None
            for flow in range(3):
                part = recvq[flow, col, rank].astype(jnp.int32).astype(jnp.float32)
                part = part * recvc[flow, col, rank]
                value = part if value is None else value + part
            total[b] = value
            even = total[b, pl.ds(0, HALF // 2, stride=2), :]
            odd = total[b, pl.ds(1, HALF // 2, stride=2), :]
            out_ref[j, :HALF // 2, :] = jnp.where(here, even, pltpu.roll(odd, BS, 1))
            out_ref[j, HALF // 2:, :] = jnp.where(here, pltpu.roll(even, BS, 1), odd)
        return carry

    lax.fori_loop(0, out_ref.shape[0] // group, settle, 0)

    for k in range(CHUNKS):
        for u in range(1, ns):
            beside(u, k).wait_send()
        for p in range(PIECES):
            for o in range(1, nt):
                across(o, k, p).wait_send()
                for u in range(1, ns):
                    forward(u, o, k, p).wait_send()

    def sent(i, carry):
        dev = lax.rem(me + i, owners)
        for copy in relayed(dev, dev):
            copy.wait_send()
        return carry

    lax.fori_loop(1, owners, sent, 0)


def local(ndp, nt, ns, activations, cotangents, block_rows, block_cols, live_counts, owner_device, owner_slot):
    ncol = nt * ns
    owners = ndp * ncol
    tokens, feats = activations.shape
    slots = block_rows.shape[1]
    cap = slots // ndp
    pair = slots // owners
    depth = tokens // CHUNKS
    dma = pltpu.SemaphoreType.DMA
    result = pl.pallas_call(
        functools.partial(kernel, ndp, nt, ns),
        out_shape=jax.ShapeDtypeStruct((cap, HALF, LANES), jnp.float32),
        in_specs=[
            pl.BlockSpec(memory_space=pltpu.VMEM),
            pl.BlockSpec(memory_space=pltpu.VMEM),
            pl.BlockSpec(memory_space=pltpu.SMEM),
            pl.BlockSpec(memory_space=pltpu.VMEM),
            pl.BlockSpec(memory_space=pltpu.VMEM),
            pl.BlockSpec(memory_space=pl.ANY),
            pl.BlockSpec(memory_space=pl.ANY),
        ],
        out_specs=pl.BlockSpec(memory_space=pltpu.VMEM),
        scratch_shapes=[
            pltpu.VMEM((8, slots), jnp.int32),
            pltpu.VMEM((8, max(cap, LANES)), jnp.int32),
            pltpu.SMEM((8, slots), jnp.int32),
            pltpu.SMEM((8, max(cap, LANES)), jnp.int32),
            pltpu.VMEM((tokens, feats), jnp.bfloat16),
            pltpu.VMEM((ncol * feats // BS, BS, depth), jnp.bfloat16),
            pltpu.VMEM((ncol * feats // BS, BS, depth), jnp.bfloat16),
            pltpu.VMEM((cotangents.shape[1] // LANES, tokens, LANES), jnp.bfloat16),
            pltpu.VMEM((slots, 2, HALF, LANES), jnp.float32),
            pltpu.VMEM((owners, pair, HALF, LANES), jnp.int16),
            pltpu.VMEM((owners, pair, 1, LANES), jnp.float32),
            pltpu.VMEM((owners, pair, HALF, LANES), jnp.int16),
            pltpu.VMEM((owners, pair, 1, LANES), jnp.float32),
            pltpu.VMEM((3, ncol, pair, HALF, LANES), jnp.int16),
            pltpu.VMEM((3, ncol, pair, 1, LANES), jnp.float32),
            pltpu.VMEM((4, HALF, LANES), jnp.float32),
            dma((cotangents.shape[1] // LANES,)),
            dma((2,)),
            dma((1 + CHUNKS,)),
            dma((ns - 1, CHUNKS)),
            dma((ns - 1, CHUNKS)),
            dma((nt - 1, CHUNKS, PIECES)),
            dma((nt - 1, CHUNKS, PIECES)),
            dma((ns - 1, nt - 1, CHUNKS, PIECES)),
            dma((ns - 1, nt - 1, CHUNKS, PIECES)),
            dma((owners,)),
            dma((owners,)),
            dma((owners,)),
            dma((owners,)),
            dma((3, ncol)),
            dma((3, ncol)),
        ],
        compiler_params=pltpu.CompilerParams(
            collective_id=0, has_side_effects=True, vmem_limit_bytes=52 * 1024 * 1024
        ),
        cost_estimate=pl.CostEstimate(flops=2 * slots * tokens * BS * LANES, bytes_accessed=16 << 20, transcendentals=0),
    )(block_rows, block_cols, live_counts, owner_device, owner_slot, activations, cotangents)
    return result.reshape(1, cap, BS * BS)


def solution(mesh):
    placed = (
        P(("groups", "dp"), ("tensor", "sub")),
        P(("groups", "dp"), ("tensor", "sub")),
        P(("tensor", "sub"), None),
        P(("tensor", "sub"), None),
        P(("tensor", "sub")),
        P(),
        P(),
    )
    return jax.shard_map(
        functools.partial(local, mesh.shape["dp"], mesh.shape["tensor"], mesh.shape["sub"]),
        mesh=mesh,
        in_specs=placed,
        out_specs=P(("groups", "dp", "tensor", "sub"), None, None),
        check_vma=False,
    )
```
